32 devices in a mesh: row: 2 (over y), col: 16 (over z, x, core).
Axes of the slice: x: 2, y: 2, z: 4, core: 2. Of those that a mesh axis runs over, the one named last changes fastest.
Arguments:
- matrix: bfloat16 [8192, 8192], P('row', 'col'), may hold values from -6 to 6
- lower_inverse: bfloat16 [2, 1024, 1024], P(None, 'row'), may hold values from -0.03125 to 0.03125
- upper_inverse: bfloat16 [2, 1024, 1024], P(None, 'row'), may hold values from -0.03125 to 0.03125
Outputs:
- factored: bfloat16 [8192, 8192], P('row', 'col')
The draws below stay inside these ranges and needn't reach their ends.
All inputs are finite; a program needn't handle non-finite values.
Results may differ from the reference program's by a relative error of at most 0.013.
Values may be sent and summed in bfloat16 or wider, within the bound.
A program may use at most 128 MiB of HBM per device.

```python
import jax
import jax.numpy as jnp
from jax import lax

NB = 1024
STEPS = 2
ORDER = 8192


def level_of(rng, extent, cuts, least, largest):
    gain = 1.0
    for dim, blocks in cuts:
        heights = jax.random.uniform(jax.random.fold_in(jax.random.fold_in(rng, 6), dim), (blocks,), jnp.float32, least / len(cuts), largest / len(cuts))
        gain = gain * jnp.repeat(jnp.exp(heights), extent[dim] // blocks).reshape((-1,) + (1,) * (len(extent) - 1 - dim))
    return gain


def centred(own_key, extent, width, most, pieces=(), held_as=jnp.bfloat16):
    array = jax.random.normal(own_key, extent, jnp.float32) * width
    if len(pieces) > 0:
        array = level_of(own_key, extent, pieces, -0.22, 0.18) * array
    return jnp.clip(array, min=-most, max=most).astype(held_as)


def setup_inputs(seed: int = 0) -> dict:
    streams_of = jax.random.split(jax.random.key(seed), 4)
    return {
        "matrix": centred(streams_of[0], (ORDER, ORDER), 1.0, 6.0, ((0, 2), (1, 16))),
        "lower_inverse": centred(streams_of[1], (STEPS, NB, NB), (32 * NB) ** -0.5, 0.03125, ((1, 2),)),
        "upper_inverse": centred(streams_of[2], (STEPS, NB, NB), (32 * NB) ** -0.5, 0.03125, ((1, 2),)),
    }


def reference(matrix, lower_inverse, upper_inverse):
    working = matrix
    for step_index in range(STEPS):
        block_low = step_index * NB
        block_high = block_low + NB
        left_panel = working[block_high:, block_low:block_high]
        column_factor = jnp.dot(left_panel, upper_inverse[step_index], preferred_element_type=jnp.float32).astype(jnp.bfloat16)
        row_factor = jnp.dot(lower_inverse[step_index], working[block_low:block_high, block_high:], preferred_element_type=jnp.float32).astype(jnp.bfloat16)
        coupling = jnp.dot(upper_inverse[step_index], row_factor, preferred_element_type=jnp.float32).astype(jnp.bfloat16)
        trail_part = working[block_high:, block_high:]
        height = trail_part.shape[0]
        blocks = trail_part.shape[1] // NB
        trail_blocks = trail_part.reshape(height, blocks, NB).transpose(1, 0, 2)
        coupling_blocks = coupling.reshape(NB, blocks, NB).transpose(1, 0, 2)

        def update(operands):
            old_block, right_block = operands
            product = jnp.dot(left_panel, right_block, preferred_element_type=jnp.float32)
            return (old_block.astype(jnp.float32) - product).astype(jnp.bfloat16)

        updated = lax.map(update, (trail_blocks, coupling_blocks))
        updated = updated.transpose(1, 0, 2).reshape(height, blocks * NB)
        working = working.at[block_high:, block_low:block_high].set(column_factor)
        working = working.at[block_low:block_high, block_high:].set(row_factor)
        working = working.at[block_high:, block_high:].set(updated)
    return working
```

```python
import functools

import jax
import jax.numpy as jnp
from jax import lax
from jax.experimental import pallas as pl
from jax.experimental.pallas import tpu as pltpu
from jax.sharding import PartitionSpec as P

NB = 1024
STEPS = 2


def spread(value, axis, root):
    mine = lax.axis_index(axis) == root
    return lax.psum(jnp.where(mine, value, jnp.zeros_like(value)), axis)


def shards(matrix, lower_inverse, upper_inverse):
    rows_local, cols_local = matrix.shape
    row_index = lax.axis_index("row")
    col_index = lax.axis_index("col")
    global_rows = row_index * rows_local + jnp.arange(rows_local, dtype=jnp.int32)[:, None]
    global_cols = col_index * cols_local + jnp.arange(cols_local, dtype=jnp.int32)[None, :]
    col_width = min(cols_local, NB)
    current = matrix
    for step_index in range(STEPS):
        block_low = step_index * NB
        block_high = block_low + NB
        owner_row = block_low // rows_local
        row_offset = block_low % rows_local
        source_rows = current[row_offset : row_offset + NB, :]
        is_owner = row_index == owner_row
        lower_full = lax.all_gather(lower_inverse[step_index], "row", axis=0, tiled=True)
        local_top = jnp.dot(lower_full, source_rows, preferred_element_type=jnp.float32).astype(
            jnp.bfloat16
        )
        masked_top = jnp.where(is_owner, local_top.astype(jnp.float32), jnp.float32(0.0))
        top_share = lax.psum_scatter(
            masked_top.astype(jnp.bfloat16), "row", scatter_dimension=0, tiled=True
        )
        top_factor = lax.all_gather(top_share, "row", axis=0, tiled=True)
        upper_start = jnp.clip(col_index * cols_local - block_low, 0, NB - col_width)
        coupling_piece = jnp.dot(
            upper_inverse[step_index], top_factor, preferred_element_type=jnp.float32
        ).astype(jnp.bfloat16)
        coupling = lax.all_gather(coupling_piece, "row", axis=0, tiled=True)
        upper_part = lax.dynamic_slice_in_dim(upper_inverse[step_index], upper_start, col_width, 1)
        upper_cols = lax.all_gather(upper_part, "row", axis=0, tiled=True)
        members = NB // cols_local
        first_root = block_low // cols_local
        panel_source = current
        panel_slabs = [
            spread(panel_source, "col", first_root + member) for member in range(members)
        ]
        whole_panel = jnp.concatenate(panel_slabs, axis=1)
        product = jnp.dot(whole_panel, coupling, preferred_element_type=jnp.float32)
        factor_sum = jnp.dot(whole_panel, upper_cols, preferred_element_type=jnp.float32)
        trailing = (current.astype(jnp.float32) - product).astype(jnp.bfloat16)
        column_factor = factor_sum.astype(jnp.bfloat16)
        placed_rows = lax.dynamic_update_slice(current, top_factor, (row_offset, 0))
        below_block = global_rows >= block_high
        right_block = global_cols >= block_high
        inside_cols = (global_cols >= block_low) & (global_cols < block_high)
        inside_rows = (global_rows >= block_low) & (global_rows < block_high)
        updated = jnp.where(below_block & right_block, trailing, current)
        updated = jnp.where(below_block & inside_cols, column_factor, updated)
        updated = jnp.where(inside_rows & right_block, placed_rows, updated)
        current = updated
    return current


CHUNK = 128
PER = 4
BLOCK = CHUNK * PER
MESH = pl.DeviceIdType.MESH


def both(*terms):
    out = terms[0]
    for term in terms[1:]:
        out = jnp.logical_and(out, term)
    return out


def fused(depth, m, lo, up, out, panel, lower_in, upper_in, factor, rows_done, own, par,
          z_sent, x_sent, c_sent, r_sent, ex_y, ex_c, ex_y_sent, ex_c_sent, f_in, f_sent):
    y = lax.axis_index("row")
    col = lax.axis_index("col")
    c = lax.rem(col, 2)
    x = lax.rem(col // 2, 2)
    z = col // 4
    width = m.shape[1]
    half = NB // 2
    quarter = half // 2
    up_z, down_z = col + 4, col - 4
    other_x = col + 2 - 4 * x
    other_c = col + 1 - 2 * c
    first = both(z == 0, x == 0)
    second = both(z == 0, x == 1)
    offset = NB * (1 - y)
    n_a = m.shape[0] // BLOCK - (NB // BLOCK) * (1 - y)
    start_b = (NB // BLOCK) * (1 - y)
    n_b = n_a - start_b

    barrier = pltpu.get_barrier_semaphore()

    def greet(target_y, target):
        pl.semaphore_signal(barrier, inc=1, device_id=(target_y, target), device_id_type=MESH)

    greet(1 - y, col)
    greet(y, other_x)
    greet(y, other_c)

    @pl.when(z > 0)
    def _():
        greet(y, down_z)

    @pl.when(z < depth - 1)
    def _():
        greet(y, up_z)

    ends = jnp.where(z == 0, 1, 0) + jnp.where(z == depth - 1, 1, 0)
    pl.semaphore_wait(barrier, 5 - ends)

    def row_of(b):
        return pl.multiple_of(offset + b * BLOCK, BLOCK)

    def piece(s, which, b, i):
        return panel.at[s, which, pl.ds(pl.multiple_of(row_of(b) + i * CHUNK, CHUNK), CHUNK), :]

    def send(s, b, i, target, sent, landed):
        ref = piece(s, c, b, i)
        return pltpu.make_async_remote_copy(
            src_ref=ref, dst_ref=ref, send_sem=sent.at[i], recv_sem=landed.at[s, b * PER + i],
            device_id=(y, target), device_id_type=MESH)

    def arrived(s, which, b, i, landed, sent):
        ref = piece(s, which, b, i)
        pltpu.make_async_remote_copy(
            src_ref=ref, dst_ref=ref, send_sem=sent.at[i], recv_sem=landed.at[s, b * PER + i],
            device_id=(y, other_c), device_id_type=MESH).wait_recv()

    def sends(s, b, i, begin):
        odd = i % 2
        act = (lambda d: d.start()) if begin else (lambda d: d.wait_send())

        @pl.when(both(z < depth - 1, x == odd))
        def _():
            act(send(s, b, i, up_z, z_sent, own))

        across = both(z > 0, x == odd)
        if s == 0 and odd == 1:
            across = jnp.logical_or(across, first)
        if s == 1 and odd == 0:
            across = jnp.logical_or(across, second)

        @pl.when(across)
        def _():
            act(send(s, b, i, other_x, x_sent, own))

        if s == 0 and odd == 0:
            @pl.when(both(z == 1, x == 1))
            def _():
                act(send(s, b, i, down_z, r_sent, own))

        if s == 0:
            act(send(s, b, i, other_c, c_sent, par))
        else:
            @pl.when(jnp.logical_not(first))
            def _():
                act(send(s, b, i, other_c, c_sent, par))

    def relay(s, b, begin_b):
        for i in range(PER):
            if s == 0:
                need = jnp.logical_not(first)
            elif i % 2 == 0:
                need = jnp.logical_not(second)
            else:
                need = z > 0

            @pl.when(need)
            def _():
                arrived(s, c, b, i, own, c_sent)

            @pl.when(b > begin_b)
            def _():
                sends(s, b - 1, i, False)

            sends(s, b, i, True)

    def drain(s, last):
        for i in range(PER):
            sends(s, last, i, False)

    def phase_a(b):
        @pl.when(first)
        def _():
            at = pl.ds(row_of(b), BLOCK)
            panel[0, c, at, :] = m[at, :]

        relay(0, b, 0)

    def product(s, b):
        at = pl.ds(row_of(b), BLOCK)
        total = jnp.dot(panel[s, 0, at, :], factor[s, :width, :], preferred_element_type=jnp.float32)
        return total + jnp.dot(
            panel[s, 1, at, :], factor[s, width:, :], preferred_element_type=jnp.float32)

    def update_0(b):
        for i in range(PER):
            arrived(0, 1 - c, b, i, par, c_sent)
        at = pl.ds(row_of(b), BLOCK)
        total = product(0, b)
        kept = m[at, :].astype(jnp.float32)
        out[at, :] = jnp.where(first, total, kept - total).astype(out.dtype)

    def update_1(b):
        @pl.when(jnp.logical_not(first))
        def _():
            for i in range(PER):
                arrived(1, 1 - c, b, i, par, c_sent)
            at = pl.ds(row_of(b), BLOCK)
            total = product(1, b)
            kept = out[at, :].astype(jnp.float32)
            out[at, :] = jnp.where(second, total, kept - total).astype(out.dtype)

    def inverse_y(item):
        s = item // 2
        src = (lo, up)[item % 2]
        dst = (lower_in, upper_in)[item % 2]
        at = pl.ds(pl.multiple_of(c * quarter, quarter), quarter)
        return pltpu.make_async_remote_copy(
            src_ref=src.at[s, at, :], dst_ref=dst.at[s, at, :], send_sem=ex_y_sent.at[item],
            recv_sem=ex_y.at[item], device_id=(1 - y, col), device_id_type=MESH)

    def inverse_c(item, which):
        s = item // 2
        dst = (lower_in, upper_in)[item % 2]
        ref = dst.at[s, pl.ds(pl.multiple_of(which * quarter, quarter), quarter), :]
        return pltpu.make_async_remote_copy(
            src_ref=ref, dst_ref=ref, send_sem=ex_c_sent.at[item],
            recv_sem=ex_c.at[item], device_id=(y, other_c), device_id_type=MESH)

    def take_inverse(item):
        inverse_y(item).wait_recv()
        inverse_c(item, c).start()
        inverse_c(item, 1 - c).wait_recv()

    def factor_y(s, part):
        ref = factor.at[s, pl.ds(part * half, half), :]
        return pltpu.make_async_remote_copy(
            src_ref=ref, dst_ref=ref, send_sem=f_sent.at[2 * s + part],
            recv_sem=f_in.at[2 * s + part], device_id=(1 - y, col), device_id_type=MESH)

    def make_rows(s):
        src = m if s == 0 else out
        at = pl.ds(s * NB, NB)
        rows_done[:half, :] = jnp.dot(
            lo[s], src[at, :], preferred_element_type=jnp.float32).astype(jnp.bfloat16)
        rows_done[half:, :] = jnp.dot(
            lower_in[s], src[at, :], preferred_element_type=jnp.float32).astype(jnp.bfloat16)
        if s == 0:
            out[at, :] = jnp.where(first, m[at, :], rows_done[...])
        else:
            @pl.when(z * 2 + x > 1)
            def _():
                out[at, :] = rows_done[...]

    def make_factor(s, part):
        src = up if part == 0 else upper_in
        at = pl.ds(part * half, half)
        inside = first if s == 0 else second

        @pl.when(jnp.logical_not(inside))
        def _():
            factor[s, at, :] = jnp.dot(
                src[s], rows_done[...], preferred_element_type=jnp.float32).astype(jnp.bfloat16)

        @pl.when(inside)
        def _():
            factor[s, at, :] = jnp.where(c == 0, src[s, :, :width], src[s, :, width:])

        factor_y(s, part).start()

    @pl.when(y == 0)
    def _():
        phase_a(0)
        take_inverse(0)
        make_rows(0)
        make_factor(0, 0)
        phase_a(1)
        take_inverse(1)
        make_factor(0, 1)

        @pl.loop(0, 2)
        def _(b):
            update_0(b)
            phase_a(b + 2)

        take_inverse(2)
        make_rows(1)
        make_factor(1, 0)

        @pl.loop(4, 6)
        def _(b):
            phase_a(b)

        take_inverse(3)
        make_factor(1, 1)

    @pl.when(y == 1)
    def _():
        inverse_y(0).start()
        inverse_y(1).start()

        @pl.loop(0, 3)
        def _(b):
            phase_a(b)

        inverse_y(0).wait_send()
        inverse_y(1).wait_send()
        inverse_y(2).start()
        inverse_y(3).start()

        @pl.loop(3, n_a)
        def _(b):
            phase_a(b)

        factor_y(0, 0).wait_recv()
        factor_y(0, 1).wait_recv()

    drain(0, n_a - 1)

    @pl.loop(0, n_b)
    def _(j):
        b = start_b + j
        later = j - n_b // 2

        @pl.when(second)
        def _():
            update_0(b)
            at = pl.ds(row_of(b), BLOCK)
            panel[1, c, at, :] = out[at, :]

        relay(1, b, start_b)

        @pl.when(both(later < 0, jnp.logical_not(second)))
        def _():
            @pl.loop(0, 2)
            def _(t):
                update_0(start_b + 2 * j + t)

        @pl.when(both(later == 0, y == 1))
        def _():
            factor_y(1, 0).wait_recv()
            factor_y(1, 1).wait_recv()

        @pl.when(later >= 0)
        def _():
            @pl.loop(0, 2)
            def _(t):
                update_1(start_b + 2 * later + t)

    drain(1, n_a - 1)

    @pl.when(y == 0)
    def _():
        for item in range(4):
            inverse_c(item, c).wait_send()
            factor_y(item // 2, item % 2).wait_send()

    @pl.when(y == 1)
    def _():
        inverse_y(2).wait_send()
        inverse_y(3).wait_send()


def streamed(depth, matrix, lower_inverse, upper_inverse):
    rows, width = matrix.shape
    half = NB // 2
    chunks = rows // CHUNK
    dma = pltpu.SemaphoreType.DMA
    return pl.pallas_call(
        functools.partial(fused, depth),
        out_shape=jax.ShapeDtypeStruct((rows, width), jnp.bfloat16),
        in_specs=[pl.BlockSpec(memory_space=pltpu.VMEM)] * 3,
        out_specs=pl.BlockSpec(memory_space=pltpu.VMEM),
        scratch_shapes=[
            pltpu.VMEM((STEPS, 2, rows, width), jnp.bfloat16),
            pltpu.VMEM((STEPS, half, NB), jnp.bfloat16),
            pltpu.VMEM((STEPS, half, NB), jnp.bfloat16),
            pltpu.VMEM((STEPS, NB, width), jnp.bfloat16),
            pltpu.VMEM((NB, width), jnp.bfloat16),
            dma((STEPS, chunks)),
            dma((STEPS, chunks)),
            dma((PER,)),
            dma((PER,)),
            dma((PER,)),
            dma((PER,)),
            dma((4,)),
            dma((4,)),
            dma((4,)),
            dma((4,)),
            dma((4,)),
            dma((4,)),
        ],
        compiler_params=pltpu.CompilerParams(
            collective_id=0, has_side_effects=True, vmem_limit_bytes=56 * 1024 * 1024),
        cost_estimate=pl.CostEstimate(
            flops=4 * rows * width * NB * STEPS, bytes_accessed=4 * rows * width, transcendentals=0),
    )(matrix, lower_inverse, upper_inverse)


def fits(mesh):
    return mesh.shape["row"] == 2 and mesh.shape["col"] == 16


def solution(mesh):
    placed = (P("row", "col"), P(None, "row", None), P(None, "row", None))
    body = functools.partial(streamed, mesh.shape["col"] // 4) if fits(mesh) else shards
    return jax.shard_map(
        body, mesh=mesh, in_specs=placed, out_specs=P("row", "col"), check_vma=False
    )
```

```python
import functools

import jax
import jax.numpy as jnp
from jax import lax
from jax.experimental import pallas as pl
from jax.experimental.pallas import tpu as pltpu
from jax.sharding import PartitionSpec as P

NB = 1024
STEPS = 2


def spread(value, axis, root):
    mine = lax.axis_index(axis) == root
    return lax.psum(jnp.where(mine, value, jnp.zeros_like(value)), axis)


def shards(matrix, lower_inverse, upper_inverse):
    rows_local, cols_local = matrix.shape
    row_index = lax.axis_index("row")
    col_index = lax.axis_index("col")
    global_rows = row_index * rows_local + jnp.arange(rows_local, dtype=jnp.int32)[:, None]
    global_cols = col_index * cols_local + jnp.arange(cols_local, dtype=jnp.int32)[None, :]
    col_width = min(cols_local, NB)
    current = matrix
    for step_index in range(STEPS):
        block_low = step_index * NB
        block_high = block_low + NB
        owner_row = block_low // rows_local
        row_offset = block_low % rows_local
        source_rows = current[row_offset : row_offset + NB, :]
        is_owner = row_index == owner_row
        lower_full = lax.all_gather(lower_inverse[step_index], "row", axis=0, tiled=True)
        local_top = jnp.dot(lower_full, source_rows, preferred_element_type=jnp.float32).astype(
            jnp.bfloat16
        )
        masked_top = jnp.where(is_owner, local_top.astype(jnp.float32), jnp.float32(0.0))
        top_share = lax.psum_scatter(
            masked_top.astype(jnp.bfloat16), "row", scatter_dimension=0, tiled=True
        )
        top_factor = lax.all_gather(top_share, "row", axis=0, tiled=True)
        upper_start = jnp.clip(col_index * cols_local - block_low, 0, NB - col_width)
        coupling_piece = jnp.dot(
            upper_inverse[step_index], top_factor, preferred_element_type=jnp.float32
        ).astype(jnp.bfloat16)
        coupling = lax.all_gather(coupling_piece, "row", axis=0, tiled=True)
        upper_part = lax.dynamic_slice_in_dim(upper_inverse[step_index], upper_start, col_width, 1)
        upper_cols = lax.all_gather(upper_part, "row", axis=0, tiled=True)
        members = NB // cols_local
        first_root = block_low // cols_local
        panel_source = current
        panel_slabs = [
            spread(panel_source, "col", first_root + member) for member in range(members)
        ]
        whole_panel = jnp.concatenate(panel_slabs, axis=1)
        product = jnp.dot(whole_panel, coupling, preferred_element_type=jnp.float32)
        factor_sum = jnp.dot(whole_panel, upper_cols, preferred_element_type=jnp.float32)
        trailing = (current.astype(jnp.float32) - product).astype(jnp.bfloat16)
        column_factor = factor_sum.astype(jnp.bfloat16)
        placed_rows = lax.dynamic_update_slice(current, top_factor, (row_offset, 0))
        below_block = global_rows >= block_high
        right_block = global_cols >= block_high
        inside_cols = (global_cols >= block_low) & (global_cols < block_high)
        inside_rows = (global_rows >= block_low) & (global_rows < block_high)
        updated = jnp.where(below_block & right_block, trailing, current)
        updated = jnp.where(below_block & inside_cols, column_factor, updated)
        updated = jnp.where(inside_rows & right_block, placed_rows, updated)
        current = updated
    return current


CHUNK = 128
PER = 4
BLOCK = CHUNK * PER
MESH = pl.DeviceIdType.MESH


def both(*terms):
    out = terms[0]
    for term in terms[1:]:
        out = jnp.logical_and(out, term)
    return out


def fused(depth, m, lo, up, out, panel, lower_in, upper_in, factor, rows_done, own, par,
          z_sent, x_sent, c_sent, r_sent, ex_y, ex_c, ex_y_sent, ex_c_sent, f_in, f_sent):
    y = lax.axis_index("row")
    col = lax.axis_index("col")
    c = lax.rem(col, 2)
    x = lax.rem(col // 2, 2)
    z = col // 4
    width = m.shape[1]
    half = NB // 2
    quarter = half // 2
    up_z, down_z = col + 4, col - 4
    other_x = col + 2 - 4 * x
    other_c = col + 1 - 2 * c
    first = both(z == 0, x == 0)
    second = both(z == 0, x == 1)
    offset = NB * (1 - y)
    n_a = m.shape[0] // BLOCK - (NB // BLOCK) * (1 - y)
    start_b = (NB // BLOCK) * (1 - y)
    n_b = n_a - start_b

    barrier = pltpu.get_barrier_semaphore()

    def greet(target_y, target):
        pl.semaphore_signal(barrier, inc=1, device_id=(target_y, target), device_id_type=MESH)

    greet(1 - y, col)
    greet(y, other_x)
    greet(y, other_c)

    @pl.when(z > 0)
    def _():
        greet(y, down_z)

    @pl.when(z < depth - 1)
    def _():
        greet(y, up_z)

    ends = jnp.where(z == 0, 1, 0) + jnp.where(z == depth - 1, 1, 0)
    pl.semaphore_wait(barrier, 5 - ends)

    def row_of(b):
        return pl.multiple_of(offset + b * BLOCK, BLOCK)

    def piece(s, which, b, i):
        return panel.at[s, which, pl.ds(pl.multiple_of(row_of(b) + i * CHUNK, CHUNK), CHUNK), :]

    def send(s, b, i, target, sent, landed):
        ref = piece(s, c, b, i)
        return pltpu.make_async_remote_copy(
            src_ref=ref, dst_ref=ref, send_sem=sent, recv_sem=landed.at[s, b * PER + i],
            device_id=(y, target), device_id_type=MESH)

    def arrived(s, which, b, i, landed):
        ref = piece(s, which, b, i)
        pltpu.make_async_remote_copy(
            src_ref=ref, dst_ref=ref, send_sem=c_sent.at[0, 0], recv_sem=landed.at[s, b * PER + i],
            device_id=(y, other_c), device_id_type=MESH).wait_recv()

    def begin(d):
        d.start()

    def finish(d):
        d.wait_send()

    def source(s):
        return first if s == 0 else second

    def chain_sends(s, b, t, act):
        i = 2 * t + x
        slot = lax.rem(b, 2) * 2 + t

        @pl.when(z < depth - 1)
        def _():
            act(send(s, b, i, up_z, z_sent.at[slot], own))

        @pl.when(z > 0)
        def _():
            act(send(s, b, i, other_x, x_sent.at[slot], own))

        @pl.when(jnp.logical_not(first) if s == 1 else True)
        def _():
            act(send(s, b, i, other_c, c_sent.at[0, slot], par))

    def cross_sends(s, b, t, act):
        i = 2 * t + 1 - x
        slot = lax.rem(b, 2) * 2 + t

        @pl.when(source(s))
        def _():
            act(send(s, b, i, other_x, x_sent.at[slot], own))

        if s == 0:
            @pl.when(both(z == 1, x == 1))
            def _():
                act(send(s, b, i, down_z, r_sent.at[slot], own))

        act(send(s, b, i, other_c, c_sent.at[1, slot], par))

    def chain(s, b, begin_b):
        for t in range(2):
            @pl.when(jnp.logical_not(source(s)))
            def _():
                arrived(s, c, b, 2 * t + x, own)

            @pl.when(b >= begin_b + 2)
            def _():
                chain_sends(s, b - 2, t, finish)

            chain_sends(s, b, t, begin)

    def cross(s, b, begin_b):
        for t in range(2):
            @pl.when(jnp.logical_not(source(s)))
            def _():
                arrived(s, c, b, 2 * t + 1 - x, own)

            @pl.when(b >= begin_b + 2)
            def _():
                cross_sends(s, b - 2, t, finish)

            cross_sends(s, b, t, begin)

    def drain(s, last):
        for b in (last - 1, last):
            for t in range(2):
                chain_sends(s, b, t, finish)

                @pl.when(jnp.logical_not(first) if s == 1 else True)
                def _():
                    cross_sends(s, b, t, finish)

    def phase_a(b, lag):
        @pl.when(b < n_a)
        def _():
            @pl.when(first)
            def _():
                at = pl.ds(row_of(b), BLOCK)
                panel[0, c, at, :] = m[at, :]

            chain(0, b, 0)

        @pl.when(both(b >= lag, b < n_a + lag))
        def _():
            cross(0, b - lag, 0)

    def product(s, b):
        at = pl.ds(row_of(b), BLOCK)
        total = jnp.dot(panel[s, 0, at, :], factor[s, :width, :], preferred_element_type=jnp.float32)
        return total + jnp.dot(
            panel[s, 1, at, :], factor[s, width:, :], preferred_element_type=jnp.float32)

    def update_0(b):
        for i in range(PER):
            arrived(0, 1 - c, b, i, par)
        at = pl.ds(row_of(b), BLOCK)
        total = product(0, b)
        kept = m[at, :].astype(jnp.float32)
        out[at, :] = jnp.where(first, total, kept - total).astype(out.dtype)

    def update_1(b):
        @pl.when(jnp.logical_not(first))
        def _():
            for i in range(PER):
                arrived(1, 1 - c, b, i, par)
            at = pl.ds(row_of(b), BLOCK)
            total = product(1, b)
            kept = out[at, :].astype(jnp.float32)
            out[at, :] = jnp.where(second, total, kept - total).astype(out.dtype)

    def inverse_y(item):
        s = item // 2
        src = (lo, up)[item % 2]
        dst = (lower_in, upper_in)[item % 2]
        at = pl.ds(pl.multiple_of(c * quarter, quarter), quarter)
        return pltpu.make_async_remote_copy(
            src_ref=src.at[s, at, :], dst_ref=dst.at[s, at, :], send_sem=ex_y_sent.at[item],
            recv_sem=ex_y.at[item], device_id=(1 - y, col), device_id_type=MESH)

    def inverse_c(item, which):
        s = item // 2
        dst = (lower_in, upper_in)[item % 2]
        ref = dst.at[s, pl.ds(pl.multiple_of(which * quarter, quarter), quarter), :]
        return pltpu.make_async_remote_copy(
            src_ref=ref, dst_ref=ref, send_sem=ex_c_sent.at[item],
            recv_sem=ex_c.at[item], device_id=(y, other_c), device_id_type=MESH)

    def take_inverse(item):
        inverse_y(item).wait_recv()
        inverse_c(item, c).start()
        inverse_c(item, 1 - c).wait_recv()

    def factor_y(s, part):
        ref = factor.at[s, pl.ds(part * half, half), :]
        return pltpu.make_async_remote_copy(
            src_ref=ref, dst_ref=ref, send_sem=f_sent.at[2 * s + part],
            recv_sem=f_in.at[2 * s + part], device_id=(1 - y, col), device_id_type=MESH)

    def make_rows(s):
        src = m if s == 0 else out
        at = pl.ds(s * NB, NB)
        rows_done[:half, :] = jnp.dot(
            lo[s], src[at, :], preferred_element_type=jnp.float32).astype(jnp.bfloat16)
        rows_done[half:, :] = jnp.dot(
            lower_in[s], src[at, :], preferred_element_type=jnp.float32).astype(jnp.bfloat16)
        if s == 0:
            out[at, :] = jnp.where(first, m[at, :], rows_done[...])
        else:
            @pl.when(z * 2 + x > 1)
            def _():
                out[at, :] = rows_done[...]

    def make_factor(s, part):
        src = up if part == 0 else upper_in
        at = pl.ds(part * half, half)
        inside = first if s == 0 else second

        @pl.when(jnp.logical_not(inside))
        def _():
            factor[s, at, :] = jnp.dot(
                src[s], rows_done[...], preferred_element_type=jnp.float32).astype(jnp.bfloat16)

        @pl.when(inside)
        def _():
            factor[s, at, :] = jnp.where(c == 0, src[s, :, :width], src[s, :, width:])

        factor_y(s, part).start()

    @pl.when(y == 0)
    def _():
        lag = jnp.where(first, 0, 2)

        @pl.loop(0, 2)
        def _(b):
            phase_a(b, lag)

        take_inverse(0)
        make_rows(0)
        make_factor(0, 0)
        phase_a(jnp.int32(2), lag)
        take_inverse(1)
        make_factor(0, 1)
        phase_a(jnp.int32(3), lag)

        @pl.loop(0, 2)
        def _(b):
            update_0(b)

        phase_a(jnp.int32(4), lag)
        take_inverse(2)
        make_rows(1)
        make_factor(1, 0)

        @pl.loop(5, 8)
        def _(b):
            phase_a(b, lag)

        take_inverse(3)
        make_factor(1, 1)

    @pl.when(y == 1)
    def _():
        lag = jnp.where(first, 0, jnp.where(second, 4, 2))
        inverse_y(0).start()
        inverse_y(1).start()

        @pl.loop(0, n_a + 4)
        def _(b):
            phase_a(b, lag)

            @pl.when(b == 3)
            def _():
                inverse_y(0).wait_send()
                inverse_y(1).wait_send()
                inverse_y(2).start()
                inverse_y(3).start()

        factor_y(0, 0).wait_recv()
        factor_y(0, 1).wait_recv()

    drain(0, n_a - 1)
    half_b = n_b // 2
    lag_b = jnp.where(second, 0, 2)

    @pl.loop(0, n_b + 2)
    def _(j):
        b = start_b + j

        @pl.when(j < n_b)
        def _():
            @pl.when(second)
            def _():
                update_0(b)
                at = pl.ds(row_of(b), BLOCK)
                panel[1, c, at, :] = out[at, :]

            chain(1, b, start_b)

        @pl.when(both(jnp.logical_not(first), j >= lag_b, j < n_b + lag_b))
        def _():
            cross(1, b - lag_b, start_b)

        @pl.when(both(j < half_b, jnp.logical_not(second)))
        def _():
            @pl.loop(0, 2)
            def _(t):
                update_0(start_b + 2 * j + t)

        @pl.when(both(j == half_b, y == 1))
        def _():
            factor_y(1, 0).wait_recv()
            factor_y(1, 1).wait_recv()

        @pl.when(j >= half_b)
        def _():
            low = jnp.where(j == half_b, 0, j - 2)

            @pl.loop(0, j - 1 - low)
            def _(t):
                update_1(start_b + low + t)

    drain(1, n_a - 1)

    @pl.when(y == 0)
    def _():
        for item in range(4):
            inverse_c(item, c).wait_send()
            factor_y(item // 2, item % 2).wait_send()

    @pl.when(y == 1)
    def _():
        inverse_y(2).wait_send()
        inverse_y(3).wait_send()


def streamed(depth, matrix, lower_inverse, upper_inverse):
    rows, width = matrix.shape
    half = NB // 2
    chunks = rows // CHUNK
    dma = pltpu.SemaphoreType.DMA
    return pl.pallas_call(
        functools.partial(fused, depth),
        out_shape=jax.ShapeDtypeStruct((rows, width), jnp.bfloat16),
        in_specs=[pl.BlockSpec(memory_space=pltpu.VMEM)] * 3,
        out_specs=pl.BlockSpec(memory_space=pltpu.VMEM),
        scratch_shapes=[
            pltpu.VMEM((STEPS, 2, rows, width), jnp.bfloat16),
            pltpu.VMEM((STEPS, half, NB), jnp.bfloat16),
            pltpu.VMEM((STEPS, half, NB), jnp.bfloat16),
            pltpu.VMEM((STEPS, NB, width), jnp.bfloat16),
            pltpu.VMEM((NB, width), jnp.bfloat16),
            dma((STEPS, chunks)),
            dma((STEPS, chunks)),
            dma((PER,)),
            dma((PER,)),
            dma((2, PER)),
            dma((PER,)),
            dma((4,)),
            dma((4,)),
            dma((4,)),
            dma((4,)),
            dma((4,)),
            dma((4,)),
        ],
        compiler_params=pltpu.CompilerParams(
            collective_id=0, has_side_effects=True, vmem_limit_bytes=56 * 1024 * 1024),
        cost_estimate=pl.CostEstimate(
            flops=4 * rows * width * NB * STEPS, bytes_accessed=4 * rows * width, transcendentals=0),
    )(matrix, lower_inverse, upper_inverse)


def fits(mesh):
    return mesh.shape["row"] == 2 and mesh.shape["col"] == 16


def solution(mesh):
    placed = (P("row", "col"), P(None, "row", None), P(None, "row", None))
    body = functools.partial(streamed, mesh.shape["col"] // 4) if fits(mesh) else shards
    return jax.shard_map(
        body, mesh=mesh, in_specs=placed, out_specs=P("row", "col"), check_vma=False
    )
```

```python
import functools

import jax
import jax.numpy as jnp
from jax import lax
from jax.experimental import pallas as pl
from jax.experimental.pallas import tpu as pltpu
from jax.sharding import PartitionSpec as P

NB = 1024
STEPS = 2


def spread(value, axis, root):
    mine = lax.axis_index(axis) == root
    return lax.psum(jnp.where(mine, value, jnp.zeros_like(value)), axis)


def shards(matrix, lower_inverse, upper_inverse):
    rows_local, cols_local = matrix.shape
    row_index = lax.axis_index("row")
    col_index = lax.axis_index("col")
    global_rows = row_index * rows_local + jnp.arange(rows_local, dtype=jnp.int32)[:, None]
    global_cols = col_index * cols_local + jnp.arange(cols_local, dtype=jnp.int32)[None, :]
    col_width = min(cols_local, NB)
    current = matrix
    for step_index in range(STEPS):
        block_low = step_index * NB
        block_high = block_low + NB
        owner_row = block_low // rows_local
        row_offset = block_low % rows_local
        source_rows = current[row_offset : row_offset + NB, :]
        is_owner = row_index == owner_row
        lower_full = lax.all_gather(lower_inverse[step_index], "row", axis=0, tiled=True)
        local_top = jnp.dot(lower_full, source_rows, preferred_element_type=jnp.float32).astype(
            jnp.bfloat16
        )
        masked_top = jnp.where(is_owner, local_top.astype(jnp.float32), jnp.float32(0.0))
        top_share = lax.psum_scatter(
            masked_top.astype(jnp.bfloat16), "row", scatter_dimension=0, tiled=True
        )
        top_factor = lax.all_gather(top_share, "row", axis=0, tiled=True)
        upper_start = jnp.clip(col_index * cols_local - block_low, 0, NB - col_width)
        coupling_piece = jnp.dot(
            upper_inverse[step_index], top_factor, preferred_element_type=jnp.float32
        ).astype(jnp.bfloat16)
        coupling = lax.all_gather(coupling_piece, "row", axis=0, tiled=True)
        upper_part = lax.dynamic_slice_in_dim(upper_inverse[step_index], upper_start, col_width, 1)
        upper_cols = lax.all_gather(upper_part, "row", axis=0, tiled=True)
        members = NB // cols_local
        first_root = block_low // cols_local
        panel_source = current
        panel_slabs = [
            spread(panel_source, "col", first_root + member) for member in range(members)
        ]
        whole_panel = jnp.concatenate(panel_slabs, axis=1)
        product = jnp.dot(whole_panel, coupling, preferred_element_type=jnp.float32)
        factor_sum = jnp.dot(whole_panel, upper_cols, preferred_element_type=jnp.float32)
        trailing = (current.astype(jnp.float32) - product).astype(jnp.bfloat16)
        column_factor = factor_sum.astype(jnp.bfloat16)
        placed_rows = lax.dynamic_update_slice(current, top_factor, (row_offset, 0))
        below_block = global_rows >= block_high
        right_block = global_cols >= block_high
        inside_cols = (global_cols >= block_low) & (global_cols < block_high)
        inside_rows = (global_rows >= block_low) & (global_rows < block_high)
        updated = jnp.where(below_block & right_block, trailing, current)
        updated = jnp.where(below_block & inside_cols, column_factor, updated)
        updated = jnp.where(inside_rows & right_block, placed_rows, updated)
        current = updated
    return current


CHUNK = 128
PER = 4
BLOCK = CHUNK * PER
MESH = pl.DeviceIdType.MESH


def both(*terms):
    out = terms[0]
    for term in terms[1:]:
        out = jnp.logical_and(out, term)
    return out


def fused(depth, m, lo, up, out, panel, lower_in, upper_in, factor, rows_done, own, par,
          z_sent, x_sent, c_sent, r_sent, ex_y, ex_c, ex_y_sent, ex_c_sent, f_in, f_sent):
    y = lax.axis_index("row")
    col = lax.axis_index("col")
    c = lax.rem(col, 2)
    x = lax.rem(col // 2, 2)
    z = col // 4
    width = m.shape[1]
    half = NB // 2
    quarter = half // 2
    up_z, down_z = col + 4, col - 4
    other_x = col + 2 - 4 * x
    other_c = col + 1 - 2 * c
    first = both(z == 0, x == 0)
    second = both(z == 0, x == 1)
    offset = NB * (1 - y)
    n_a = m.shape[0] // BLOCK - (NB // BLOCK) * (1 - y)
    start_b = (NB // BLOCK) * (1 - y)
    n_b = n_a - start_b

    barrier = pltpu.get_barrier_semaphore()

    def greet(target_y, target):
        pl.semaphore_signal(barrier, inc=1, device_id=(target_y, target), device_id_type=MESH)

    greet(1 - y, col)
    greet(y, other_x)
    greet(y, other_c)

    @pl.when(z > 0)
    def _():
        greet(y, down_z)

    @pl.when(z < depth - 1)
    def _():
        greet(y, up_z)

    ends = jnp.where(z == 0, 1, 0) + jnp.where(z == depth - 1, 1, 0)
    pl.semaphore_wait(barrier, 5 - ends)

    def row_of(b):
        return pl.multiple_of(offset + b * BLOCK, BLOCK)

    def piece(s, which, b, i):
        return panel.at[s, which, pl.ds(pl.multiple_of(row_of(b) + i * CHUNK, CHUNK), CHUNK), :]

    def send(s, b, i, target, sent, landed):
        ref = piece(s, c, b, i)
        return pltpu.make_async_remote_copy(
            src_ref=ref, dst_ref=ref, send_sem=sent, recv_sem=landed.at[s, b * PER + i],
            device_id=(y, target), device_id_type=MESH)

    def arrived(s, which, b, i, landed):
        ref = piece(s, which, b, i)
        pltpu.make_async_remote_copy(
            src_ref=ref, dst_ref=ref, send_sem=c_sent.at[0, 0], recv_sem=landed.at[s, b * PER + i],
            device_id=(y, other_c), device_id_type=MESH).wait_recv()

    def begin(d):
        d.start()

    def finish(d):
        d.wait_send()

    def source(s):
        return first if s == 0 else second

    def chain_sends(s, b, t, act):
        i = 2 * t + x
        slot = lax.rem(b, 2) * 2 + t

        @pl.when(z < depth - 1)
        def _():
            act(send(s, b, i, up_z, z_sent.at[slot], own))

        @pl.when(z > 0)
        def _():
            act(send(s, b, i, other_x, x_sent.at[slot], own))

        @pl.when(jnp.logical_not(first) if s == 1 else True)
        def _():
            act(send(s, b, i, other_c, c_sent.at[0, slot], par))

    def cross_sends(s, b, t, act):
        i = 2 * t + 1 - x
        slot = lax.rem(b, 2) * 2 + t

        @pl.when(source(s))
        def _():
            act(send(s, b, i, other_x, x_sent.at[slot], own))

        if s == 0:
            @pl.when(both(z == 1, x == 1))
            def _():
                act(send(s, b, i, down_z, r_sent.at[slot], own))

        act(send(s, b, i, other_c, c_sent.at[1, slot], par))

    def chain(s, b, begin_b):
        for t in range(2):
            @pl.when(jnp.logical_not(source(s)))
            def _():
                arrived(s, c, b, 2 * t + x, own)

            @pl.when(b >= begin_b + 2)
            def _():
                chain_sends(s, b - 2, t, finish)

            chain_sends(s, b, t, begin)

    def cross(s, b, begin_b):
        for t in range(2):
            @pl.when(jnp.logical_not(source(s)))
            def _():
                arrived(s, c, b, 2 * t + 1 - x, own)

            @pl.when(b >= begin_b + 2)
            def _():
                cross_sends(s, b - 2, t, finish)

            cross_sends(s, b, t, begin)

    def drain(s, last):
        for b in (last - 1, last):
            for t in range(2):
                chain_sends(s, b, t, finish)

                @pl.when(jnp.logical_not(first) if s == 1 else True)
                def _():
                    cross_sends(s, b, t, finish)

    def phase_a(b, lag):
        @pl.when(b < n_a)
        def _():
            @pl.when(first)
            def _():
                at = pl.ds(row_of(b), BLOCK)
                panel[0, c, at, :] = m[at, :]

            chain(0, b, 0)

        @pl.when(both(b >= lag, b < n_a + lag))
        def _():
            cross(0, b - lag, 0)

    def product(s, b):
        at = pl.ds(row_of(b), BLOCK)
        total = jnp.dot(panel[s, 0, at, :], factor[s, :width, :], preferred_element_type=jnp.float32)
        return total + jnp.dot(
            panel[s, 1, at, :], factor[s, width:, :], preferred_element_type=jnp.float32)

    def update_0(b):
        for i in range(PER):
            arrived(0, 1 - c, b, i, par)
        at = pl.ds(row_of(b), BLOCK)
        total = product(0, b)
        kept = m[at, :].astype(jnp.float32)
        out[at, :] = jnp.where(first, total, kept - total).astype(out.dtype)

    def update_1(b):
        @pl.when(jnp.logical_not(first))
        def _():
            for i in range(PER):
                arrived(1, 1 - c, b, i, par)
            at = pl.ds(row_of(b), BLOCK)
            total = product(1, b)
            kept = out[at, :].astype(jnp.float32)
            out[at, :] = jnp.where(second, total, kept - total).astype(out.dtype)

    def inverse_y(item):
        s = item // 2
        src = (lo, up)[item % 2]
        dst = (lower_in, upper_in)[item % 2]
        at = pl.ds(pl.multiple_of(c * quarter, quarter), quarter)
        return pltpu.make_async_remote_copy(
            src_ref=src.at[s, at, :], dst_ref=dst.at[s, at, :], send_sem=ex_y_sent.at[item],
            recv_sem=ex_y.at[item], device_id=(1 - y, col), device_id_type=MESH)

    def inverse_c(item, which):
        s = item // 2
        dst = (lower_in, upper_in)[item % 2]
        ref = dst.at[s, pl.ds(pl.multiple_of(which * quarter, quarter), quarter), :]
        return pltpu.make_async_remote_copy(
            src_ref=ref, dst_ref=ref, send_sem=ex_c_sent.at[item],
            recv_sem=ex_c.at[item], device_id=(y, other_c), device_id_type=MESH)

    def take_inverse(item):
        inverse_y(item).wait_recv()
        inverse_c(item, c).start()
        inverse_c(item, 1 - c).wait_recv()

    def factor_y(s, part):
        ref = factor.at[s, pl.ds(part * half, half), :]
        return pltpu.make_async_remote_copy(
            src_ref=ref, dst_ref=ref, send_sem=f_sent.at[2 * s + part],
            recv_sem=f_in.at[2 * s + part], device_id=(1 - y, col), device_id_type=MESH)

    def make_rows(s):
        src = m if s == 0 else out
        at = pl.ds(s * NB, NB)
        rows_done[:half, :] = jnp.dot(
            lo[s], src[at, :], preferred_element_type=jnp.float32).astype(jnp.bfloat16)
        rows_done[half:, :] = jnp.dot(
            lower_in[s], src[at, :], preferred_element_type=jnp.float32).astype(jnp.bfloat16)
        if s == 0:
            out[at, :] = jnp.where(first, m[at, :], rows_done[...])
        else:
            @pl.when(z * 2 + x > 1)
            def _():
                out[at, :] = rows_done[...]

    def make_factor(s, part):
        src = up if part == 0 else upper_in
        at = pl.ds(part * half, half)
        inside = first if s == 0 else second

        @pl.when(jnp.logical_not(inside))
        def _():
            factor[s, at, :] = jnp.dot(
                src[s], rows_done[...], preferred_element_type=jnp.float32).astype(jnp.bfloat16)

        @pl.when(inside)
        def _():
            factor[s, at, :] = jnp.where(c == 0, src[s, :, :width], src[s, :, width:])

        factor_y(s, part).start()

    @pl.when(y == 0)
    def _():
        lag = jnp.where(first, 0, 2)

        phase_a(jnp.int32(0), lag)

        @pl.when(z == 0)
        def _():
            phase_a(jnp.int32(1), lag)

        take_inverse(0)
        make_rows(0)
        make_factor(0, 0)

        @pl.when(z > 0)
        def _():
            phase_a(jnp.int32(1), lag)

        take_inverse(1)
        make_factor(0, 1)

        @pl.loop(2, 4)
        def _(b):
            phase_a(b, lag)

        @pl.loop(0, 2)
        def _(b):
            update_0(b)

        phase_a(jnp.int32(4), lag)
        take_inverse(2)
        make_rows(1)
        make_factor(1, 0)

        @pl.loop(5, 8)
        def _(b):
            phase_a(b, lag)

        take_inverse(3)
        make_factor(1, 1)

    @pl.when(y == 1)
    def _():
        lag = jnp.where(first, 0, jnp.where(second, 4, 2))
        inverse_y(0).start()
        hold = jnp.where(z == 0, 2, 0)

        @pl.loop(0, n_a + 4)
        def _(b):
            phase_a(b, lag)

            for item in range(1, 4):
                @pl.when(b == hold + 2 * (item - 1))
                def _():
                    inverse_y(item - 1).wait_send()
                    inverse_y(item).start()

        factor_y(0, 0).wait_recv()
        factor_y(0, 1).wait_recv()

    drain(0, n_a - 1)
    half_b = n_b // 2
    lag_b = jnp.where(second, 0, 2)

    @pl.loop(0, n_b + 2)
    def _(j):
        b = start_b + j

        @pl.when(j < n_b)
        def _():
            @pl.when(second)
            def _():
                update_0(b)
                at = pl.ds(row_of(b), BLOCK)
                panel[1, c, at, :] = out[at, :]

            chain(1, b, start_b)

        @pl.when(both(jnp.logical_not(first), j >= lag_b, j < n_b + lag_b))
        def _():
            cross(1, b - lag_b, start_b)

        @pl.when(both(j < half_b, jnp.logical_not(second)))
        def _():
            @pl.loop(0, 2)
            def _(t):
                update_0(start_b + 2 * j + t)

        @pl.when(both(j == half_b, y == 1))
        def _():
            factor_y(1, 0).wait_recv()
            factor_y(1, 1).wait_recv()

        @pl.when(j >= half_b)
        def _():
            low = jnp.where(j == half_b, 0, j - 2)

            @pl.loop(0, j - 1 - low)
            def _(t):
                update_1(start_b + low + t)

    drain(1, n_a - 1)

    @pl.when(y == 0)
    def _():
        for item in range(4):
            inverse_c(item, c).wait_send()
            factor_y(item // 2, item % 2).wait_send()

    @pl.when(y == 1)
    def _():
        inverse_y(3).wait_send()


def streamed(depth, matrix, lower_inverse, upper_inverse):
    rows, width = matrix.shape
    half = NB // 2
    chunks = rows // CHUNK
    dma = pltpu.SemaphoreType.DMA
    return pl.pallas_call(
        functools.partial(fused, depth),
        out_shape=jax.ShapeDtypeStruct((rows, width), jnp.bfloat16),
        in_specs=[pl.BlockSpec(memory_space=pltpu.VMEM)] * 3,
        out_specs=pl.BlockSpec(memory_space=pltpu.VMEM),
        scratch_shapes=[
            pltpu.VMEM((STEPS, 2, rows, width), jnp.bfloat16),
            pltpu.VMEM((STEPS, half, NB), jnp.bfloat16),
            pltpu.VMEM((STEPS, half, NB), jnp.bfloat16),
            pltpu.VMEM((STEPS, NB, width), jnp.bfloat16),
            pltpu.VMEM((NB, width), jnp.bfloat16),
            dma((STEPS, chunks)),
            dma((STEPS, chunks)),
            dma((PER,)),
            dma((PER,)),
            dma((2, PER)),
            dma((PER,)),
            dma((4,)),
            dma((4,)),
            dma((4,)),
            dma((4,)),
            dma((4,)),
            dma((4,)),
        ],
        compiler_params=pltpu.CompilerParams(
            collective_id=0, has_side_effects=True, vmem_limit_bytes=56 * 1024 * 1024),
        cost_estimate=pl.CostEstimate(
            flops=4 * rows * width * NB * STEPS, bytes_accessed=4 * rows * width, transcendentals=0),
    )(matrix, lower_inverse, upper_inverse)


def fits(mesh):
    return mesh.shape["row"] == 2 and mesh.shape["col"] == 16


def solution(mesh):
    placed = (P("row", "col"), P(None, "row", None), P(None, "row", None))
    body = functools.partial(streamed, mesh.shape["col"] // 4) if fits(mesh) else shards
    return jax.shard_map(
        body, mesh=mesh, in_specs=placed, out_specs=P("row", "col"), check_vma=False
    )
```

```python
import functools

import jax
import jax.numpy as jnp
from jax import lax
from jax.experimental import pallas as pl
from jax.experimental.pallas import tpu as pltpu
from jax.sharding import PartitionSpec as P

NB = 1024
STEPS = 2


def spread(value, axis, root):
    mine = lax.axis_index(axis) == root
    return lax.psum(jnp.where(mine, value, jnp.zeros_like(value)), axis)


def shards(matrix, lower_inverse, upper_inverse):
    rows_local, cols_local = matrix.shape
    row_index = lax.axis_index("row")
    col_index = lax.axis_index("col")
    global_rows = row_index * rows_local + jnp.arange(rows_local, dtype=jnp.int32)[:, None]
    global_cols = col_index * cols_local + jnp.arange(cols_local, dtype=jnp.int32)[None, :]
    col_width = min(cols_local, NB)
    current = matrix
    for step_index in range(STEPS):
        block_low = step_index * NB
        block_high = block_low + NB
        owner_row = block_low // rows_local
        row_offset = block_low % rows_local
        source_rows = current[row_offset : row_offset + NB, :]
        is_owner = row_index == owner_row
        lower_full = lax.all_gather(lower_inverse[step_index], "row", axis=0, tiled=True)
        local_top = jnp.dot(lower_full, source_rows, preferred_element_type=jnp.float32).astype(
            jnp.bfloat16
        )
        masked_top = jnp.where(is_owner, local_top.astype(jnp.float32), jnp.float32(0.0))
        top_share = lax.psum_scatter(
            masked_top.astype(jnp.bfloat16), "row", scatter_dimension=0, tiled=True
        )
        top_factor = lax.all_gather(top_share, "row", axis=0, tiled=True)
        upper_start = jnp.clip(col_index * cols_local - block_low, 0, NB - col_width)
        coupling_piece = jnp.dot(
            upper_inverse[step_index], top_factor, preferred_element_type=jnp.float32
        ).astype(jnp.bfloat16)
        coupling = lax.all_gather(coupling_piece, "row", axis=0, tiled=True)
        upper_part = lax.dynamic_slice_in_dim(upper_inverse[step_index], upper_start, col_width, 1)
        upper_cols = lax.all_gather(upper_part, "row", axis=0, tiled=True)
        members = NB // cols_local
        first_root = block_low // cols_local
        panel_source = current
        panel_slabs = [
            spread(panel_source, "col", first_root + member) for member in range(members)
        ]
        whole_panel = jnp.concatenate(panel_slabs, axis=1)
        product = jnp.dot(whole_panel, coupling, preferred_element_type=jnp.float32)
        factor_sum = jnp.dot(whole_panel, upper_cols, preferred_element_type=jnp.float32)
        trailing = (current.astype(jnp.float32) - product).astype(jnp.bfloat16)
        column_factor = factor_sum.astype(jnp.bfloat16)
        placed_rows = lax.dynamic_update_slice(current, top_factor, (row_offset, 0))
        below_block = global_rows >= block_high
        right_block = global_cols >= block_high
        inside_cols = (global_cols >= block_low) & (global_cols < block_high)
        inside_rows = (global_rows >= block_low) & (global_rows < block_high)
        updated = jnp.where(below_block & right_block, trailing, current)
        updated = jnp.where(below_block & inside_cols, column_factor, updated)
        updated = jnp.where(inside_rows & right_block, placed_rows, updated)
        current = updated
    return current


CHUNK = 128
PER = 4
BLOCK = CHUNK * PER
MESH = pl.DeviceIdType.MESH


def both(*terms):
    out = terms[0]
    for term in terms[1:]:
        out = jnp.logical_and(out, term)
    return out


def fused(depth, m, lo, up, out, panel, lower_in, upper_in, factor, rows_done, own, par,
          z_sent, x_sent, c_sent, r_sent, ex_y, ex_c, ex_y_sent, ex_c_sent, f_in, f_sent):
    y = lax.axis_index("row")
    col = lax.axis_index("col")
    c = lax.rem(col, 2)
    x = lax.rem(col // 2, 2)
    z = col // 4
    width = m.shape[1]
    half = NB // 2
    quarter = half // 2
    up_z, down_z = col + 4, col - 4
    other_x = col + 2 - 4 * x
    other_c = col + 1 - 2 * c
    first = both(z == 0, x == 0)
    second = both(z == 0, x == 1)
    offset = NB * (1 - y)
    n_a = m.shape[0] // BLOCK - (NB // BLOCK) * (1 - y)
    start_b = (NB // BLOCK) * (1 - y)
    n_b = n_a - start_b

    barrier = pltpu.get_barrier_semaphore()

    def greet(target_y, target):
        pl.semaphore_signal(barrier, inc=1, device_id=(target_y, target), device_id_type=MESH)

    greet(1 - y, col)
    greet(y, other_x)
    greet(y, other_c)

    @pl.when(z > 0)
    def _():
        greet(y, down_z)

    @pl.when(z < depth - 1)
    def _():
        greet(y, up_z)

    ends = jnp.where(z == 0, 1, 0) + jnp.where(z == depth - 1, 1, 0)
    pl.semaphore_wait(barrier, 5 - ends)

    def row_of(b):
        return pl.multiple_of(offset + b * BLOCK, BLOCK)

    def piece(s, which, b, i):
        return panel.at[s, which, pl.ds(pl.multiple_of(row_of(b) + i * CHUNK, CHUNK), CHUNK), :]

    def send(s, b, i, target, sent, landed):
        ref = piece(s, c, b, i)
        return pltpu.make_async_remote_copy(
            src_ref=ref, dst_ref=ref, send_sem=sent, recv_sem=landed.at[s, b * PER + i],
            device_id=(y, target), device_id_type=MESH)

    def arrived(s, which, b, i, landed):
        ref = piece(s, which, b, i)
        pltpu.make_async_remote_copy(
            src_ref=ref, dst_ref=ref, send_sem=c_sent.at[0, 0], recv_sem=landed.at[s, b * PER + i],
            device_id=(y, other_c), device_id_type=MESH).wait_recv()

    def begin(d):
        d.start()

    def finish(d):
        d.wait_send()

    def source(s):
        return first if s == 0 else second

    def chain_sends(s, b, t, act):
        i = 2 * t + x
        slot = lax.rem(b, 2) * 2 + t

        @pl.when(z < depth - 1)
        def _():
            act(send(s, b, i, up_z, z_sent.at[slot], own))

        @pl.when(z > 0)
        def _():
            act(send(s, b, i, other_x, x_sent.at[slot], own))

        @pl.when(jnp.logical_not(first) if s == 1 else True)
        def _():
            act(send(s, b, i, other_c, c_sent.at[0, slot], par))

    def cross_sends(s, b, t, act):
        i = 2 * t + 1 - x
        slot = lax.rem(b, 2) * 2 + t

        @pl.when(source(s))
        def _():
            act(send(s, b, i, other_x, x_sent.at[slot], own))

        if s == 0:
            @pl.when(both(z == 1, x == 1))
            def _():
                act(send(s, b, i, down_z, r_sent.at[slot], own))

        act(send(s, b, i, other_c, c_sent.at[1, slot], par))

    def chain(s, b, begin_b):
        for t in range(2):
            @pl.when(jnp.logical_not(source(s)))
            def _():
                arrived(s, c, b, 2 * t + x, own)

            @pl.when(b >= begin_b + 2)
            def _():
                chain_sends(s, b - 2, t, finish)

            chain_sends(s, b, t, begin)

    def cross(s, b, begin_b):
        for t in range(2):
            @pl.when(jnp.logical_not(source(s)))
            def _():
                arrived(s, c, b, 2 * t + 1 - x, own)

            @pl.when(b >= begin_b + 2)
            def _():
                cross_sends(s, b - 2, t, finish)

            cross_sends(s, b, t, begin)

    def drain(s, last):
        for b in (last - 1, last):
            for t in range(2):
                chain_sends(s, b, t, finish)

                @pl.when(jnp.logical_not(first) if s == 1 else True)
                def _():
                    cross_sends(s, b, t, finish)

    def phase_a(b, lag):
        @pl.when(b < n_a)
        def _():
            @pl.when(first)
            def _():
                at = pl.ds(row_of(b), BLOCK)
                panel[0, c, at, :] = m[at, :]

            chain(0, b, 0)

        @pl.when(both(b >= lag, b < n_a + lag))
        def _():
            cross(0, b - lag, 0)

    def product(s, b):
        at = pl.ds(row_of(b), BLOCK)
        total = jnp.dot(panel[s, 0, at, :], factor[s, :width, :], preferred_element_type=jnp.float32)
        return total + jnp.dot(
            panel[s, 1, at, :], factor[s, width:, :], preferred_element_type=jnp.float32)

    def update_0(b):
        for i in range(PER):
            arrived(0, 1 - c, b, i, par)
        at = pl.ds(row_of(b), BLOCK)
        total = product(0, b)
        kept = m[at, :].astype(jnp.float32)
        out[at, :] = jnp.where(first, total, kept - total).astype(out.dtype)

    def update_1(b):
        @pl.when(jnp.logical_not(first))
        def _():
            for i in range(PER):
                arrived(1, 1 - c, b, i, par)
            at = pl.ds(row_of(b), BLOCK)
            total = product(1, b)
            kept = out[at, :].astype(jnp.float32)
            out[at, :] = jnp.where(second, total, kept - total).astype(out.dtype)

    def inverse_y(item):
        s = item // 2
        src = (lo, up)[item % 2]
        dst = (lower_in, upper_in)[item % 2]
        at = pl.ds(pl.multiple_of(c * quarter, quarter), quarter)
        return pltpu.make_async_remote_copy(
            src_ref=src.at[s, at, :], dst_ref=dst.at[s, at, :], send_sem=ex_y_sent.at[item],
            recv_sem=ex_y.at[item], device_id=(1 - y, col), device_id_type=MESH)

    def inverse_c(item, which):
        s = item // 2
        dst = (lower_in, upper_in)[item % 2]
        ref = dst.at[s, pl.ds(pl.multiple_of(which * quarter, quarter), quarter), :]
        return pltpu.make_async_remote_copy(
            src_ref=ref, dst_ref=ref, send_sem=ex_c_sent.at[item],
            recv_sem=ex_c.at[item], device_id=(y, other_c), device_id_type=MESH)

    def take_inverse(item):
        inverse_y(item).wait_recv()
        inverse_c(item, c).start()
        inverse_c(item, 1 - c).wait_recv()

    def factor_y(s, part):
        ref = factor.at[s, pl.ds(part * half, half), :]
        return pltpu.make_async_remote_copy(
            src_ref=ref, dst_ref=ref, send_sem=f_sent.at[2 * s + part],
            recv_sem=f_in.at[2 * s + part], device_id=(1 - y, col), device_id_type=MESH)

    def make_rows(s):
        src = m if s == 0 else out
        at = pl.ds(s * NB, NB)
        rows_done[:half, :] = jnp.dot(
            lo[s], src[at, :], preferred_element_type=jnp.float32).astype(jnp.bfloat16)
        rows_done[half:, :] = jnp.dot(
            lower_in[s], src[at, :], preferred_element_type=jnp.float32).astype(jnp.bfloat16)
        out[at, :] = rows_done[...]

    def make_factor(s, part):
        src = up if part == 0 else upper_in
        at = pl.ds(part * half, half)
        inside = source(s)

        @pl.when(jnp.logical_not(jnp.logical_or(first, inside)))
        def _():
            factor[s, at, :] = jnp.dot(
                src[s], rows_done[...], preferred_element_type=jnp.float32).astype(jnp.bfloat16)

        @pl.when(inside)
        def _():
            factor[s, at, :] = jnp.where(c == 0, src[s, :, :width], src[s, :, width:])

        @pl.when(jnp.logical_not(first) if s == 1 else True)
        def _():
            factor_y(s, part).start()

    @pl.when(y == 0)
    def _():
        lag = jnp.where(first, 0, jnp.where(second, 3, 2))
        ahead = jnp.where(first, n_a, jnp.where(z == 0, 3, 2))
        middle = jnp.maximum(ahead, 2 + lag)

        @pl.loop(0, ahead)
        def _(b):
            phase_a(b, lag)

        take_inverse(0)

        @pl.when(jnp.logical_not(first))
        def _():
            make_rows(0)

        @pl.when(first)
        def _():
            out[:NB, :] = m[:NB, :]

        make_factor(0, 0)
        take_inverse(1)
        make_factor(0, 1)

        @pl.loop(0, middle - ahead)
        def _(t):
            phase_a(ahead + t, lag)

        @pl.loop(0, 2)
        def _(b):
            update_0(b)

        @pl.loop(0, n_a + lag - middle)
        def _(t):
            phase_a(middle + t, lag)

        take_inverse(2)

        @pl.when(z * 2 + x > 1)
        def _():
            make_rows(1)

        make_factor(1, 0)
        take_inverse(3)
        make_factor(1, 1)

    @pl.when(y == 1)
    def _():
        lag = jnp.where(first, 0, jnp.where(second, 4, 2))
        hold = jnp.where(z == 0, 3, 1)
        inverse_y(0).start()
        inverse_y(1).start()

        @pl.loop(0, n_a + 4)
        def _(b):
            phase_a(b, lag)

            @pl.when(b == hold)
            def _():
                inverse_y(0).wait_send()
                inverse_y(1).wait_send()
                inverse_y(2).start()
                inverse_y(3).start()

        factor_y(0, 0).wait_recv()
        factor_y(0, 1).wait_recv()

    drain(0, n_a - 1)
    half_b = n_b // 2
    turn = half_b + y
    lag_b = jnp.where(second, 0, 2)

    @pl.loop(0, n_b + 2)
    def _(j):
        b = start_b + j

        @pl.when(j < n_b)
        def _():
            @pl.when(second)
            def _():
                update_0(b)
                at = pl.ds(row_of(b), BLOCK)
                panel[1, c, at, :] = out[at, :]

            chain(1, b, start_b)

        @pl.when(both(jnp.logical_not(first), j >= lag_b, j < n_b + lag_b))
        def _():
            cross(1, b - lag_b, start_b)

        @pl.when(both(j < half_b, jnp.logical_not(second)))
        def _():
            @pl.loop(0, 2)
            def _(t):
                update_0(start_b + 2 * j + t)

        @pl.when(both(j == turn, y == 1, jnp.logical_not(first)))
        def _():
            factor_y(1, 0).wait_recv()
            factor_y(1, 1).wait_recv()

        @pl.when(j >= turn)
        def _():
            low = jnp.where(j == turn, 0, jnp.minimum(j - 2, 2 * (j - turn) + 1))
            high = jnp.minimum(j - 1, 2 * (j - turn) + 3)

            @pl.loop(0, high - low)
            def _(t):
                update_1(start_b + low + t)

    drain(1, n_a - 1)

    @pl.when(y == 0)
    def _():
        for item in range(4):
            inverse_c(item, c).wait_send()

            @pl.when(jnp.logical_not(first) if item > 1 else True)
            def _():
                factor_y(item // 2, item % 2).wait_send()

    @pl.when(y == 1)
    def _():
        inverse_y(2).wait_send()
        inverse_y(3).wait_send()


def streamed(depth, matrix, lower_inverse, upper_inverse):
    rows, width = matrix.shape
    half = NB // 2
    chunks = rows // CHUNK
    dma = pltpu.SemaphoreType.DMA
    return pl.pallas_call(
        functools.partial(fused, depth),
        out_shape=jax.ShapeDtypeStruct((rows, width), jnp.bfloat16),
        in_specs=[pl.BlockSpec(memory_space=pltpu.VMEM)] * 3,
        out_specs=pl.BlockSpec(memory_space=pltpu.VMEM),
        scratch_shapes=[
            pltpu.VMEM((STEPS, 2, rows, width), jnp.bfloat16),
            pltpu.VMEM((STEPS, half, NB), jnp.bfloat16),
            pltpu.VMEM((STEPS, half, NB), jnp.bfloat16),
            pltpu.VMEM((STEPS, NB, width), jnp.bfloat16),
            pltpu.VMEM((NB, width), jnp.bfloat16),
            dma((STEPS, chunks)),
            dma((STEPS, chunks)),
            dma((PER,)),
            dma((PER,)),
            dma((2, PER)),
            dma((PER,)),
            dma((4,)),
            dma((4,)),
            dma((4,)),
            dma((4,)),
            dma((4,)),
            dma((4,)),
        ],
        compiler_params=pltpu.CompilerParams(
            collective_id=0, has_side_effects=True, vmem_limit_bytes=56 * 1024 * 1024),
        cost_estimate=pl.CostEstimate(
            flops=4 * rows * width * NB * STEPS, bytes_accessed=4 * rows * width, transcendentals=0),
    )(matrix, lower_inverse, upper_inverse)


def fits(mesh):
    return mesh.shape["row"] == 2 and mesh.shape["col"] == 16


def solution(mesh):
    placed = (P("row", "col"), P(None, "row", None), P(None, "row", None))
    body = functools.partial(streamed, mesh.shape["col"] // 4) if fits(mesh) else shards
    return jax.shard_map(
        body, mesh=mesh, in_specs=placed, out_specs=P("row", "col"), check_vma=False
    )
```

```python
import functools

import jax
import jax.numpy as jnp
from jax import lax
from jax.experimental import pallas as pl
from jax.experimental.pallas import tpu as pltpu
from jax.sharding import PartitionSpec as P

NB = 1024
STEPS = 2


def spread(value, axis, root):
    mine = lax.axis_index(axis) == root
    return lax.psum(jnp.where(mine, value, jnp.zeros_like(value)), axis)


def shards(matrix, lower_inverse, upper_inverse):
    rows_local, cols_local = matrix.shape
    row_index = lax.axis_index("row")
    col_index = lax.axis_index("col")
    global_rows = row_index * rows_local + jnp.arange(rows_local, dtype=jnp.int32)[:, None]
    global_cols = col_index * cols_local + jnp.arange(cols_local, dtype=jnp.int32)[None, :]
    col_width = min(cols_local, NB)
    current = matrix
    for step_index in range(STEPS):
        block_low = step_index * NB
        block_high = block_low + NB
        owner_row = block_low // rows_local
        row_offset = block_low % rows_local
        source_rows = current[row_offset : row_offset + NB, :]
        is_owner = row_index == owner_row
        lower_full = lax.all_gather(lower_inverse[step_index], "row", axis=0, tiled=True)
        local_top = jnp.dot(lower_full, source_rows, preferred_element_type=jnp.float32).astype(
            jnp.bfloat16
        )
        masked_top = jnp.where(is_owner, local_top.astype(jnp.float32), jnp.float32(0.0))
        top_share = lax.psum_scatter(
            masked_top.astype(jnp.bfloat16), "row", scatter_dimension=0, tiled=True
        )
        top_factor = lax.all_gather(top_share, "row", axis=0, tiled=True)
        upper_start = jnp.clip(col_index * cols_local - block_low, 0, NB - col_width)
        coupling_piece = jnp.dot(
            upper_inverse[step_index], top_factor, preferred_element_type=jnp.float32
        ).astype(jnp.bfloat16)
        coupling = lax.all_gather(coupling_piece, "row", axis=0, tiled=True)
        upper_part = lax.dynamic_slice_in_dim(upper_inverse[step_index], upper_start, col_width, 1)
        upper_cols = lax.all_gather(upper_part, "row", axis=0, tiled=True)
        members = NB // cols_local
        first_root = block_low // cols_local
        panel_source = current
        panel_slabs = [
            spread(panel_source, "col", first_root + member) for member in range(members)
        ]
        whole_panel = jnp.concatenate(panel_slabs, axis=1)
        product = jnp.dot(whole_panel, coupling, preferred_element_type=jnp.float32)
        factor_sum = jnp.dot(whole_panel, upper_cols, preferred_element_type=jnp.float32)
        trailing = (current.astype(jnp.float32) - product).astype(jnp.bfloat16)
        column_factor = factor_sum.astype(jnp.bfloat16)
        placed_rows = lax.dynamic_update_slice(current, top_factor, (row_offset, 0))
        below_block = global_rows >= block_high
        right_block = global_cols >= block_high
        inside_cols = (global_cols >= block_low) & (global_cols < block_high)
        inside_rows = (global_rows >= block_low) & (global_rows < block_high)
        updated = jnp.where(below_block & right_block, trailing, current)
        updated = jnp.where(below_block & inside_cols, column_factor, updated)
        updated = jnp.where(inside_rows & right_block, placed_rows, updated)
        current = updated
    return current


CHUNK = 128
PER = 4
BLOCK = CHUNK * PER
MESH = pl.DeviceIdType.MESH


def both(*terms):
    out = terms[0]
    for term in terms[1:]:
        out = jnp.logical_and(out, term)
    return out


def fused(depth, m, lo, up, out, panel, lower_in, upper_in, factor, rows_done, own, par,
          z_sent, x_sent, c_sent, r_sent, ex_y, ex_c, ex_y_sent, ex_c_sent, f_in, f_sent):
    y = lax.axis_index("row")
    col = lax.axis_index("col")
    c = lax.rem(col, 2)
    x = lax.rem(col // 2, 2)
    z = col // 4
    width = m.shape[1]
    half = NB // 2
    quarter = half // 2
    up_z, down_z = col + 4, col - 4
    other_x = col + 2 - 4 * x
    other_c = col + 1 - 2 * c
    first = both(z == 0, x == 0)
    second = both(z == 0, x == 1)
    offset = NB * (1 - y)
    n_a = m.shape[0] // BLOCK - (NB // BLOCK) * (1 - y)
    start_b = (NB // BLOCK) * (1 - y)
    n_b = n_a - start_b

    barrier = pltpu.get_barrier_semaphore()

    def greet(target_y, target):
        pl.semaphore_signal(barrier, inc=1, device_id=(target_y, target), device_id_type=MESH)

    greet(1 - y, col)
    greet(y, other_x)
    greet(y, other_c)

    @pl.when(z > 0)
    def _():
        greet(y, down_z)

    @pl.when(z < depth - 1)
    def _():
        greet(y, up_z)

    ends = jnp.where(z == 0, 1, 0) + jnp.where(z == depth - 1, 1, 0)
    pl.semaphore_wait(barrier, 5 - ends)

    def row_of(b):
        return pl.multiple_of(offset + b * BLOCK, BLOCK)

    def piece(s, which, b, i):
        return panel.at[s, which, pl.ds(pl.multiple_of(row_of(b) + i * CHUNK, CHUNK), CHUNK), :]

    def send(s, b, i, target, sent, landed):
        ref = piece(s, c, b, i)
        return pltpu.make_async_remote_copy(
            src_ref=ref, dst_ref=ref, send_sem=sent, recv_sem=landed.at[s, b * PER + i],
            device_id=(y, target), device_id_type=MESH)

    def arrived(s, which, b, i, landed):
        ref = piece(s, which, b, i)
        pltpu.make_async_remote_copy(
            src_ref=ref, dst_ref=ref, send_sem=c_sent.at[0, 0], recv_sem=landed.at[s, b * PER + i],
            device_id=(y, other_c), device_id_type=MESH).wait_recv()

    def begin(d):
        d.start()

    def finish(d):
        d.wait_send()

    def source(s):
        return first if s == 0 else second

    def chain_sends(s, b, t, act):
        i = 2 * t + x
        slot = lax.rem(b, 2) * 2 + t

        @pl.when(z < depth - 1)
        def _():
            act(send(s, b, i, up_z, z_sent.at[slot], own))

        @pl.when(z > 0)
        def _():
            act(send(s, b, i, other_x, x_sent.at[slot], own))

        @pl.when(jnp.logical_not(first) if s == 1 else True)
        def _():
            act(send(s, b, i, other_c, c_sent.at[2 * s, slot], par))

    def cross_sends(s, b, t, act):
        i = 2 * t + 1 - x
        slot = lax.rem(b, 2) * 2 + t

        @pl.when(source(s))
        def _():
            act(send(s, b, i, other_x, x_sent.at[slot], own))

        if s == 0:
            @pl.when(both(z == 1, x == 1))
            def _():
                act(send(s, b, i, down_z, r_sent.at[slot], own))

        act(send(s, b, i, other_c, c_sent.at[2 * s + 1, slot], par))

    def chain(s, b, begin_b):
        for t in range(2):
            @pl.when(jnp.logical_not(source(s)))
            def _():
                arrived(s, c, b, 2 * t + x, own)

            @pl.when(b >= begin_b + 2)
            def _():
                chain_sends(s, b - 2, t, finish)

            chain_sends(s, b, t, begin)

    def cross(s, b, begin_b):
        for t in range(2):
            @pl.when(jnp.logical_not(source(s)))
            def _():
                arrived(s, c, b, 2 * t + 1 - x, own)

            @pl.when(b >= begin_b + 2)
            def _():
                cross_sends(s, b - 2, t, finish)

            cross_sends(s, b, t, begin)

    def drain(s, last, chains, crosses):
        for b in (last - 1, last):
            for t in range(2):
                @pl.when(chains)
                def _():
                    chain_sends(s, b, t, finish)

                @pl.when(crosses)
                def _():
                    cross_sends(s, b, t, finish)

    def phase_a(b, lag):
        @pl.when(b < n_a)
        def _():
            @pl.when(first)
            def _():
                at = pl.ds(row_of(b), BLOCK)
                panel[0, c, at, :] = m[at, :]

            chain(0, b, 0)

        @pl.when(both(b >= lag, b < n_a + lag))
        def _():
            cross(0, b - lag, 0)

    def product(s, b):
        at = pl.ds(row_of(b), BLOCK)
        total = jnp.dot(panel[s, 0, at, :], factor[s, :width, :], preferred_element_type=jnp.float32)
        return total + jnp.dot(
            panel[s, 1, at, :], factor[s, width:, :], preferred_element_type=jnp.float32)

    def update_0(b):
        for i in range(PER):
            arrived(0, 1 - c, b, i, par)
        at = pl.ds(row_of(b), BLOCK)
        total = product(0, b)
        kept = m[at, :].astype(jnp.float32)
        out[at, :] = jnp.where(first, total, kept - total).astype(out.dtype)

    def update_1(b):
        @pl.when(jnp.logical_not(first))
        def _():
            for i in range(PER):
                arrived(1, 1 - c, b, i, par)
            at = pl.ds(row_of(b), BLOCK)
            total = product(1, b)
            kept = out[at, :].astype(jnp.float32)
            out[at, :] = jnp.where(second, total, kept - total).astype(out.dtype)

    def inverse_y(item):
        s = item // 2
        src = (lo, up)[item % 2]
        dst = (lower_in, upper_in)[item % 2]
        at = pl.ds(pl.multiple_of(c * quarter, quarter), quarter)
        return pltpu.make_async_remote_copy(
            src_ref=src.at[s, at, :], dst_ref=dst.at[s, at, :], send_sem=ex_y_sent.at[item],
            recv_sem=ex_y.at[item], device_id=(1 - y, col), device_id_type=MESH)

    def inverse_c(item, which):
        s = item // 2
        dst = (lower_in, upper_in)[item % 2]
        ref = dst.at[s, pl.ds(pl.multiple_of(which * quarter, quarter), quarter), :]
        return pltpu.make_async_remote_copy(
            src_ref=ref, dst_ref=ref, send_sem=ex_c_sent.at[item],
            recv_sem=ex_c.at[item], device_id=(y, other_c), device_id_type=MESH)

    def take_inverse(item):
        inverse_y(item).wait_recv()
        inverse_c(item, c).start()
        inverse_c(item, 1 - c).wait_recv()

    def factor_y(s, part):
        ref = factor.at[s, pl.ds(part * half, half), :]
        return pltpu.make_async_remote_copy(
            src_ref=ref, dst_ref=ref, send_sem=f_sent.at[2 * s + part],
            recv_sem=f_in.at[2 * s + part], device_id=(1 - y, col), device_id_type=MESH)

    def make_rows(s):
        src = m if s == 0 else out
        at = pl.ds(s * NB, NB)
        rows_done[:half, :] = jnp.dot(
            lo[s], src[at, :], preferred_element_type=jnp.float32).astype(jnp.bfloat16)
        rows_done[half:, :] = jnp.dot(
            lower_in[s], src[at, :], preferred_element_type=jnp.float32).astype(jnp.bfloat16)
        out[at, :] = rows_done[...]

    def make_factor(s, part):
        src = up if part == 0 else upper_in
        at = pl.ds(part * half, half)
        inside = source(s)

        @pl.when(jnp.logical_not(jnp.logical_or(first, inside)))
        def _():
            factor[s, at, :] = jnp.dot(
                src[s], rows_done[...], preferred_element_type=jnp.float32).astype(jnp.bfloat16)

        @pl.when(inside)
        def _():
            factor[s, at, :] = jnp.where(c == 0, src[s, :, :width], src[s, :, width:])

        @pl.when(jnp.logical_not(first) if s == 1 else True)
        def _():
            factor_y(s, part).start()

    @pl.when(y == 0)
    def _():
        lag = jnp.where(first, 0, jnp.where(second, 3, 2))
        ahead = jnp.where(first, n_a, jnp.where(z == 0, 3, 2))
        middle = jnp.maximum(ahead, 2 + lag)

        @pl.loop(0, ahead)
        def _(b):
            phase_a(b, lag)

        take_inverse(0)

        @pl.when(jnp.logical_not(first))
        def _():
            make_rows(0)

        @pl.when(first)
        def _():
            out[:NB, :] = m[:NB, :]

        make_factor(0, 0)
        take_inverse(1)
        make_factor(0, 1)

        @pl.loop(0, middle - ahead)
        def _(t):
            phase_a(ahead + t, lag)

        @pl.loop(0, 2)
        def _(b):
            update_0(b)

        @pl.loop(0, n_a + lag - middle)
        def _(t):
            phase_a(middle + t, lag)

        take_inverse(2)

        @pl.when(z * 2 + x > 1)
        def _():
            make_rows(1)

        make_factor(1, 0)
        take_inverse(3)
        make_factor(1, 1)

    @pl.when(y == 1)
    def _():
        lag = jnp.where(first, 0, jnp.where(second, 4, 2))
        hold = jnp.where(z == 0, 3, 1)
        inverse_y(0).start()
        inverse_y(1).start()

        @pl.loop(0, jnp.where(second, n_a, n_a + 2))
        def _(b):
            phase_a(b, lag)

            @pl.when(b == hold)
            def _():
                inverse_y(0).wait_send()
                inverse_y(1).wait_send()
                inverse_y(2).start()
                inverse_y(3).start()

        factor_y(0, 0).wait_recv()
        factor_y(0, 1).wait_recv()

    eager = both(second, y == 1)
    drain(0, n_a - 1, True, jnp.logical_not(eager))
    half_b = n_b // 2
    turn = jnp.where(second, n_b, half_b + y)
    lag_b = jnp.where(second, 0, 2)

    @pl.loop(0, n_b + 2)
    def _(j):
        b = start_b + j

        @pl.when(j < n_b)
        def _():
            @pl.when(second)
            def _():
                update_0(b)
                at = pl.ds(row_of(b), BLOCK)
                panel[1, c, at, :] = out[at, :]

            chain(1, b, start_b)

        @pl.when(both(jnp.logical_not(first), j >= lag_b, j < n_b + lag_b))
        def _():
            cross(1, b - lag_b, start_b)

        @pl.when(both(eager, j < 4))
        def _():
            cross(0, n_a - 4 + j, 0)

        @pl.when(both(j < half_b, jnp.logical_not(second)))
        def _():
            @pl.loop(0, 2)
            def _(t):
                update_0(start_b + 2 * j + t)

        @pl.when(both(j == turn, y == 1, jnp.logical_not(first)))
        def _():
            factor_y(1, 0).wait_recv()
            factor_y(1, 1).wait_recv()

        @pl.when(j >= turn)
        def _():
            low = jnp.where(j == turn, 0, jnp.minimum(j - 2, 2 * (j - turn) + 1))
            high = jnp.minimum(j - 1, 2 * (j - turn) + 3)

            low = jnp.where(second, 0, low)
            high = jnp.where(second, jnp.where(j == n_b, n_b, 0), high)

            @pl.loop(0, high - low)
            def _(t):
                update_1(start_b + low + t)

    drain(0, n_a - 1, False, eager)
    drain(1, n_a - 1, True, jnp.logical_not(first))

    @pl.when(y == 0)
    def _():
        for item in range(4):
            inverse_c(item, c).wait_send()

            @pl.when(jnp.logical_not(first) if item > 1 else True)
            def _():
                factor_y(item // 2, item % 2).wait_send()

    @pl.when(y == 1)
    def _():
        inverse_y(2).wait_send()
        inverse_y(3).wait_send()


def streamed(depth, matrix, lower_inverse, upper_inverse):
    rows, width = matrix.shape
    half = NB // 2
    chunks = rows // CHUNK
    dma = pltpu.SemaphoreType.DMA
    return pl.pallas_call(
        functools.partial(fused, depth),
        out_shape=jax.ShapeDtypeStruct((rows, width), jnp.bfloat16),
        in_specs=[pl.BlockSpec(memory_space=pltpu.VMEM)] * 3,
        out_specs=pl.BlockSpec(memory_space=pltpu.VMEM),
        scratch_shapes=[
            pltpu.VMEM((STEPS, 2, rows, width), jnp.bfloat16),
            pltpu.VMEM((STEPS, half, NB), jnp.bfloat16),
            pltpu.VMEM((STEPS, half, NB), jnp.bfloat16),
            pltpu.VMEM((STEPS, NB, width), jnp.bfloat16),
            pltpu.VMEM((NB, width), jnp.bfloat16),
            dma((STEPS, chunks)),
            dma((STEPS, chunks)),
            dma((PER,)),
            dma((PER,)),
            dma((2 * STEPS, PER)),
            dma((PER,)),
            dma((4,)),
            dma((4,)),
            dma((4,)),
            dma((4,)),
            dma((4,)),
            dma((4,)),
        ],
        compiler_params=pltpu.CompilerParams(
            collective_id=0, has_side_effects=True, vmem_limit_bytes=56 * 1024 * 1024),
        cost_estimate=pl.CostEstimate(
            flops=4 * rows * width * NB * STEPS, bytes_accessed=4 * rows * width, transcendentals=0),
    )(matrix, lower_inverse, upper_inverse)


def fits(mesh):
    return mesh.shape["row"] == 2 and mesh.shape["col"] == 16


def solution(mesh):
    placed = (P("row", "col"), P(None, "row", None), P(None, "row", None))
    body = functools.partial(streamed, mesh.shape["col"] // 4) if fits(mesh) else shards
    return jax.shard_map(
        body, mesh=mesh, in_specs=placed, out_specs=P("row", "col"), check_vma=False
    )
```
